32 devices in a mesh: groups: 2 (over y), lat: 4 (over z), lon: 2 (over x), feat: 2 (over core).
Axes of the slice: x: 2, y: 2, z: 4, core: 2. Of those that a mesh axis runs over, the one named last changes fastest.
Arguments:
- grid_latent: bfloat16 [32768, 512], P(('groups', 'lat', 'lon'), 'feat'), parts along dimension 0, may hold values from -6 to 6
- teacher: bfloat16 [32768, 512], P(('groups', 'lat', 'lon'), 'feat'), parts along dimension 0, may hold values from -6 to 6
- mesh_init: bfloat16 [5120, 512], P(('groups', 'lat', 'lon'), 'feat'), parts along dimension 0, may hold values from -6 to 6
- enc_weight: bfloat16 [512, 512], P(None, 'feat'), may hold values from -0.25 to 0.25
- proc_weight: bfloat16 [512, 512], P(None, 'feat'), may hold values from -0.25 to 0.25
- dec_weight: bfloat16 [512, 512], P(None, 'feat'), may hold values from -0.25 to 0.25
- local_grid: int32 [16384], P(('lat', 'lon')), may hold values from 0 to 2047
- local_mesh: int32 [16384], P(('lat', 'lon')), may hold values from 0 to 319
- local_weight: float32 [16384], P(('lat', 'lon')), may hold values from 0.2 to 1
- send_row: int32 [40, 256], P(('lat', 'lon')), may hold values from 0 to 2047
- send_count: int32 [40], P(('lat', 'lon')), may hold values from 0 to 256, as said below
- recv_row: int32 [40, 256], P(('lat', 'lon')), may hold values from 0 to 319
- recv_weight: float32 [40, 256], P(('lat', 'lon')), may hold values from 0.2 to 1
- coarse_index: int32 [2560, 2], P(('lat', 'lon')), may hold values from 0 to 31
- coarse_weight: float32 [2560, 2], P(('lat', 'lon')), may hold values from -3 to 3
Outputs:
- loss_value: float32 [2], P('groups'), parts along dimension 0
- grad_x: bfloat16 [32768, 512], P(('groups', 'lat', 'lon'), 'feat'), parts along dimension 0
- grad_dec: float32 [1024, 512], P(('groups', 'lat', 'lon'), 'feat'), parts along dimension 0
The draws below stay inside these ranges and needn't reach their ends.
There are 2 independent parts, one for each index of `groups`. The reference program is written for one: setup_inputs(seed, part) draws one part's arguments, and reference() takes and returns one part's arrays. A program takes and returns all parts, laid end to end along the dimension named above; an argument that names none is the same for every part. Nothing has to cross between parts.
Inputs may be any that keep to these rules, and one draw needn't show every extreme that they name: send_count[s * 5 + k] is 0 exactly where the target band of neighbour k does not exist; otherwise at least 1. The bucket to neighbour (0,1) and every bucket of the first and last bands are full wherever the target exists.
All inputs are finite; a program needn't handle non-finite values.
Results may differ from the reference program's by a relative error of at most 0.0067.
Values may be sent and summed in bfloat16 or wider, within the bound.
A program may use at most 64 MiB of HBM per device.

```python
import jax
import jax.numpy as jnp
from jax import lax

L = 512
GDEV = 2048
MDEV = 320
CDEV = 4
KC = 2
NB = 5
CAP = 256
SHARDS = 8
EDGES_DEV = 2048
GRID = 16384
MESH = 2560
COARSE = 32
EDGES = 16384
N_LAT = 4
N_LON = 2


def draw_send_count(key, part):
    key = jax.random.fold_in(key, 11)
    counts = jax.random.randint(key, (N_LAT, N_LON, NB), 1, CAP + 1)
    band_ids = jnp.arange(N_LAT)[:, None, None]
    slot_ids = jnp.arange(NB)[None, None, :]
    polar_band = (band_ids == 0) | (band_ids == N_LAT - 1)
    counts = jnp.where(polar_band | (slot_ids == 3), CAP, counts)
    band_shift = jnp.array([-1, 1, -1, 0, 1])[None, None, :]
    target = band_ids + band_shift
    counts = jnp.where((target >= 0) & (target < N_LAT), counts, 0)
    return counts.reshape(-1).astype(jnp.int32)


def place_ends(values, key, least, top_value):
    shape = values.shape
    spot = [jax.random.randint(jax.random.fold_in(key, axis), (), 0, shape[axis]) for axis in range(len(shape))]
    values = values.at[tuple(spot)].set(least)
    longest = shape.index(max(shape))
    spot[longest] = (spot[longest] + 1) % shape[longest]
    return values.at[tuple(spot)].set(top_value)


def shard_levels(rng, dims, split, low, largest):
    def one(position, shards_of):
        heights = jax.random.uniform(jax.random.fold_in(jax.random.fold_in(rng, 6), position), (shards_of,), jnp.float32, low / len(split), largest / len(split))
        return jnp.repeat(jnp.exp(heights), dims[position] // shards_of).reshape((-1,) + (1,) * (len(dims) - position - 1))

    gain = one(*split[0])
    for cut in split[1:]:
        gain = gain * one(*cut)
    return gain


def noise(own_key, dims, scale, bound, pieces=(), kind=jnp.bfloat16):
    drawn = scale * jax.random.normal(own_key, dims, jnp.float32)
    if pieces:
        drawn = drawn * shard_levels(own_key, dims, pieces, -0.22, 0.18)
    return jnp.clip(drawn, -bound, bound).astype(kind)


def setup_inputs(seed: int = 0, part: int = 0) -> dict:
    streams_of = jax.random.split(jax.random.key(seed), 16)
    own_keys = jax.random.split(jax.random.fold_in(streams_of[15], part), 16)
    grid_latent = noise(own_keys[0], (GRID, L), 1.0, 6.0, ((0, 8), (1, 2)))
    teacher = noise(own_keys[1], (GRID, L), 1.0, 6.0, ((0, 8), (1, 2)))
    mesh_init = noise(own_keys[2], (MESH, L), 1.0, 6.0, ((0, 8), (1, 2)))
    enc_weight = noise(streams_of[3], (L, L), L ** -0.5, 0.25, ((1, 2),))
    proc_weight = noise(streams_of[4], (L, L), L ** -0.5, 0.25, ((1, 2),))
    dec_weight = noise(streams_of[5], (L, L), L ** -0.5, 0.25, ((1, 2),))
    local_grid = place_ends(jax.random.randint(streams_of[6], (EDGES,), 0, GDEV), jax.random.fold_in(streams_of[6], 1), 0, GDEV - 1).astype(jnp.int32)
    local_mesh = place_ends(jax.random.randint(streams_of[7], (EDGES,), 0, MDEV), jax.random.fold_in(streams_of[7], 1), 0, MDEV - 1).astype(jnp.int32)
    local_weight = jnp.clip(0.2 + 0.8 * jax.random.uniform(streams_of[8], (EDGES,), jnp.float32) ** shard_levels(streams_of[8], (EDGES,), ((0, 8),), -0.2, 0.2), 0.2, 1.0)
    send_row = place_ends(jax.random.randint(streams_of[9], (SHARDS * NB, CAP), 0, GDEV), jax.random.fold_in(streams_of[9], 1), 0, GDEV - 1).astype(jnp.int32)
    send_count = draw_send_count(jax.random.fold_in(streams_of[15], 71), part)
    recv_row = place_ends(jax.random.randint(streams_of[11], (SHARDS * NB, CAP), 0, MDEV), jax.random.fold_in(streams_of[11], 1), 0, MDEV - 1).astype(jnp.int32)
    recv_weight = jnp.clip(0.2 + 0.8 * jax.random.uniform(streams_of[12], (SHARDS * NB, CAP), jnp.float32) ** shard_levels(streams_of[12], (SHARDS * NB, CAP), ((0, 8),), -0.2, 0.2), 0.2, 1.0)
    coarse_index = place_ends(jax.random.randint(streams_of[13], (MESH, KC), 0, COARSE), jax.random.fold_in(streams_of[13], 1), 0, COARSE - 1).astype(jnp.int32)
    coarse_weight = noise(streams_of[14], (MESH, KC), 0.5, 3.0, ((0, 8),), jnp.float32)
    return {"grid_latent": grid_latent, "teacher": teacher, "mesh_init": mesh_init, "enc_weight": enc_weight, "proc_weight": proc_weight, "dec_weight": dec_weight, "local_grid": local_grid, "local_mesh": local_mesh, "local_weight": local_weight, "send_row": send_row, "send_count": send_count, "recv_row": recv_row, "recv_weight": recv_weight, "coarse_index": coarse_index, "coarse_weight": coarse_weight}


OFFSETS = ((-1, 0), (1, 0), (-1, 1), (0, 1), (1, 1))


def silu_slope(pre_value):
    sigma = jax.nn.sigmoid(pre_value)
    return sigma * (1.0 + pre_value * (1.0 - sigma))


def edge_tables(local_grid, local_mesh, send_row, send_count, recv_row, recv_weight):
    shards = N_LAT * N_LON
    owner_shard = (jnp.arange(shards * EDGES_DEV) // EDGES_DEV).astype(jnp.int32)
    local_from = owner_shard * GDEV + local_grid
    local_to = owner_shard * MDEV + local_mesh
    sender = (jnp.arange(shards * NB) // NB).astype(jnp.int32)
    neighbour = (jnp.arange(shards * NB) % NB).astype(jnp.int32)
    lat_shift = jnp.array([offset_pair[0] for offset_pair in OFFSETS], jnp.int32)[neighbour]
    lon_shift = jnp.array([offset_pair[1] for offset_pair in OFFSETS], jnp.int32)[neighbour]
    to_band = sender // N_LON + lat_shift
    sector = (sender % N_LON + lon_shift) % N_LON
    target = jnp.clip(to_band, 0, N_LAT - 1) * N_LON + sector
    table_row = target * NB + neighbour
    slot_ids = jnp.arange(CAP, dtype=jnp.int32)
    band_ok = (to_band >= 0) & (to_band < N_LAT)
    live_mask = (slot_ids[None, :] < send_count[:, None]) & band_ok[:, None]
    remote_from = (sender * GDEV)[:, None] + send_row
    remote_to = (target * MDEV)[:, None] + recv_row[table_row]
    remote_weight = jnp.where(live_mask, recv_weight[table_row], 0.0)
    return local_from, local_to, remote_from.reshape(-1), remote_to.reshape(-1), remote_weight.reshape(-1)


def reference(grid_latent, teacher, mesh_init, enc_weight, proc_weight, dec_weight, local_grid, local_mesh, local_weight, send_row, send_count, recv_row, recv_weight, coarse_index, coarse_weight):
    shards = N_LAT * N_LON
    grid_total = GDEV * shards
    mesh_total = MDEV * shards
    local_from, local_to, remote_from, remote_to, remote_weight = edge_tables(local_grid, local_mesh, send_row, send_count, recv_row, recv_weight)

    def to_mesh(grid_values):
        local_part = jax.ops.segment_sum(local_weight[:, None] * grid_values[local_from].astype(jnp.float32), local_to, num_segments=mesh_total)
        remote_part = jax.ops.segment_sum(remote_weight[:, None] * grid_values[remote_from].astype(jnp.float32), remote_to, num_segments=mesh_total)
        return local_part + remote_part

    def to_grid(mesh_values):
        local_part = jax.ops.segment_sum(local_weight[:, None] * mesh_values[local_to], local_from, num_segments=grid_total)
        messages = (remote_weight[:, None] * mesh_values[remote_to]).astype(jnp.bfloat16)
        messages = lax.optimization_barrier(messages).astype(jnp.float32)
        remote_part = jax.ops.segment_sum(messages, remote_from, num_segments=grid_total)
        return local_part + remote_part

    pre_enc = jnp.dot(grid_latent, enc_weight, preferred_element_type=jnp.float32)
    encoded = jax.nn.silu(pre_enc).astype(jnp.bfloat16)
    mesh_state = (mesh_init.astype(jnp.float32) + to_mesh(encoded)).astype(jnp.bfloat16)
    pre_proc = jnp.dot(mesh_state, proc_weight, preferred_element_type=jnp.float32)
    processed = jax.nn.silu(pre_proc).astype(jnp.bfloat16)
    coarse_all = processed.reshape(shards, MDEV, L)[:, :CDEV].reshape(shards * CDEV, L)
    linked = coarse_all[coarse_index].astype(jnp.float32)
    long_range = jnp.sum(coarse_weight[:, :, None] * linked, axis=1)
    updated = (mesh_state.astype(jnp.float32) + processed.astype(jnp.float32) + long_range).astype(jnp.bfloat16)
    pre_dec = jnp.dot(updated, dec_weight, preferred_element_type=jnp.float32)
    decoded = jax.nn.silu(pre_dec)
    student = grid_latent.astype(jnp.float32) + to_grid(decoded)
    row_ids = jnp.arange(grid_total).astype(jnp.float32)
    area_weight = 0.25 + jnp.sin(jnp.pi * (row_ids + 0.5) / grid_total)
    target = teacher.astype(jnp.float32)
    residual = student - target
    misfit = jnp.sum(area_weight[:, None] * residual * residual)
    energy = jnp.sum(area_weight[:, None] * target * target)
    loss_value = (misfit / energy).reshape(1)
    slope_full = 2.0 * area_weight[:, None] * residual / energy
    slope_half = slope_full.astype(jnp.bfloat16)
    back_decoded = to_mesh(slope_half)
    grad_pre_dec = (back_decoded * silu_slope(pre_dec)).astype(jnp.bfloat16)
    grad_dec = jnp.dot(updated.T, grad_pre_dec, preferred_element_type=jnp.float32)
    back_updated = jnp.dot(grad_pre_dec, dec_weight.T, preferred_element_type=jnp.float32)
    coarse_terms = jax.ops.segment_sum((coarse_weight[:, :, None] * back_updated[:, None, :]).reshape(-1, L), coarse_index.reshape(-1), num_segments=shards * CDEV)
    coarse_block = jnp.pad(coarse_terms.reshape(shards, CDEV, L), ((0, 0), (0, MDEV - CDEV), (0, 0))).reshape(mesh_total, L)
    back_processed = back_updated + coarse_block
    grad_pre_proc = (back_processed * silu_slope(pre_proc)).astype(jnp.bfloat16)
    back_mesh = back_updated + jnp.dot(grad_pre_proc, proc_weight.T, preferred_element_type=jnp.float32)
    back_encoded = to_grid(back_mesh)
    grad_pre_enc = (back_encoded * silu_slope(pre_enc)).astype(jnp.bfloat16)
    grad_x = (slope_full + jnp.dot(grad_pre_enc, enc_weight.T, preferred_element_type=jnp.float32)).astype(jnp.bfloat16)
    return loss_value, grad_x, grad_dec
```

```python
import functools

import jax
import jax.numpy as jnp
from jax import lax
from jax.experimental import pallas as pl
from jax.experimental.pallas import tpu as pltpu
from jax.sharding import PartitionSpec as P

CDEV = 4
PAD = 8
TILE = 256
OFFSETS = ((-1, 0), (1, 0), (-1, 1), (0, 1), (1, 1))
NB = len(OFFSETS)
MESH_ID = pl.DeviceIdType.MESH
F32 = jnp.float32
BF16 = jnp.bfloat16


def silu(v):
    return v * jax.nn.sigmoid(v)


def silu_slope(v):
    q = jax.nn.sigmoid(v)
    return q * (1.0 + v * (1.0 - q))


def nn(a, b):
    return jnp.dot(a, b, preferred_element_type=F32)


def nt(a, b):
    return lax.dot_general(a, b, (((1,), (1,)), ((), ())), preferred_element_type=F32)


def tn(a, b):
    return lax.dot_general(a, b, (((0,), (0,)), ((), ())), preferred_element_type=F32)


def iota(shape, dim):
    return lax.broadcasted_iota(jnp.int32, shape, dim)


def kernel(
    nlat, nlon, scatter_here,
    grid_ref, teach_ref, init_ref, encw_ref, procw_ref, decw_ref, area_ref,
    lg_row, lm_row, lw_row, sr_row, sr_col, rr_row, rr_col, rw_row, rw_col,
    ci_col, ci_row, cw_col, cw_row,
    loss_ref, gx_ref, gd_ref,
    xo, enco, proco, deco,
    mw, gt, am, amt, sm, smt, rm, rmt, cm, cmt,
    pre_enc, enc, slope, slope_half, gpe, gpeo, back,
    bsend, brecv,
    state, stateo, pre_proc, proc_v, upd, updo, pre_dec, gpd, gpdo, bu, bp, gpp, gppo,
    ebuf, mbuf, cbuf, tbuf, rbuf, pg, gbuf,
    psend, precv, rsend, rrecv, esend, erecv, msend, mrecv, csend, crecv, tsend, trecv, gsend, grecv,
):
    b = lax.axis_index("lat")
    o = lax.axis_index("lon")
    f = lax.axis_index("feat")
    nd = nlat * nlon * 2
    shards = nlat * nlon
    sid = b * nlon + o
    me = sid * 2 + f
    rows, width = grid_ref.shape
    mrows = init_ref.shape[0]
    cap = rr_col.shape[0] // NB
    tiles = rows // TILE
    own = pl.ds(pl.multiple_of(f * width, width), width)
    oth = pl.ds(pl.multiple_of((1 - f) * width, width), width)

    def tile(t):
        return pl.ds(pl.multiple_of(t * TILE, TILE), TILE)

    def loop(n, body, start=0):
        lax.fori_loop(start, n, lambda i, c: (body(i), c)[1], 0)

    barrier = pltpu.get_barrier_semaphore()

    def greet(r):
        d = lax.rem(me + r, nd)
        pl.semaphore_signal(
            barrier, inc=1, device_id_type=MESH_ID,
            device_id={"lat": d // (2 * nlon), "lon": lax.rem(d // 2, nlon), "feat": lax.rem(d, 2)},
        )

    loop(nd, greet, 1)
    pl.semaphore_wait(barrier, nd - 1)

    def partner(src, dst, i):
        return pltpu.make_async_remote_copy(
            src_ref=src, dst_ref=dst, send_sem=psend.at[i], recv_sem=precv.at[i],
            device_id={"feat": 1 - f}, device_id_type=MESH_ID,
        )

    def x_copy(t):
        return partner(grid_ref.at[tile(t)], xo.at[tile(t)], t)

    def g_copy(t):
        return partner(gpe.at[tile(t)], gpeo.at[tile(t)], tiles + t)

    base = 2 * tiles
    w_copies = [
        partner(decw_ref.at[oth], deco, base),
        partner(procw_ref.at[oth], proco, base + 1),
        partner(encw_ref.at[oth], enco, base + 2),
    ]
    loop(tiles, lambda t: x_copy(t).start())
    for c in w_copies:
        c.start()

    def spread(buf_from, buf_to, ss, rs, count, scatter):
        whole_group = count == nd
        mine = me if whole_group else sid

        def copy(r):
            d = lax.rem(mine + r, count)
            src = buf_from(d) if scatter else buf_from(mine)
            if whole_group:
                where = {"lat": d // (2 * nlon), "lon": lax.rem(d // 2, nlon), "feat": lax.rem(d, 2)}
            else:
                where = {"lat": d // nlon, "lon": lax.rem(d, nlon)}
            return pltpu.make_async_remote_copy(
                src_ref=src, dst_ref=buf_to.at[mine], send_sem=ss.at[d], recv_sem=rs.at[mine],
                device_id=where, device_id_type=MESH_ID,
            )

        def arrival(r):
            d = lax.rem(mine + r, count)
            return pltpu.make_async_remote_copy(
                src_ref=buf_to.at[d], dst_ref=buf_to.at[d], send_sem=ss.at[d], recv_sem=rs.at[d],
                device_id={"feat": 1 - f}, device_id_type=MESH_ID,
            )

        return (
            lambda: loop(count, lambda r: copy(r).start(), 1),
            lambda: loop(count, lambda r: arrival(r).wait_recv(), 1),
            lambda: loop(count, lambda r: copy(r).wait_send(), 1),
        )

    e_start, e_recv, e_sent = spread(lambda i: ebuf.at[i], ebuf, esend, erecv, nd, False)
    m_start, m_recv, m_sent = spread(lambda i: mbuf.at[i], mbuf, msend, mrecv, nd, False)
    c_start, c_recv, c_sent = spread(lambda i: cbuf.at[i], cbuf, csend, crecv, shards, False)
    t_start, t_recv, t_sent = spread(lambda i: tbuf.at[i], rbuf, tsend, trecv, shards, True)

    def route_copy(phase, k, direction):
        db, do = OFFSETS[k]
        return pltpu.make_async_remote_copy(
            src_ref=bsend.at[phase, k], dst_ref=brecv.at[phase, k],
            send_sem=rsend.at[phase, k], recv_sem=rrecv.at[phase, k],
            device_id={"lat": b + direction * db, "lon": lax.rem(o + direction * do + nlon, nlon)},
            device_id_type=MESH_ID,
        )

    def when_band(step, fn):
        if step == 0:
            fn()
        elif step > 0:
            pl.when(b < nlat - 1)(fn)
        else:
            pl.when(b > 0)(fn)

    def no_band(step, fn):
        if step > 0:
            pl.when(b == nlat - 1)(fn)
        elif step < 0:
            pl.when(b == 0)(fn)

    ORDER = (2, 4, 3, 0, 1)

    def route_start(phase, k, direction):
        when_band(direction * OFFSETS[k][0], lambda: route_copy(phase, k, direction).start())

    def route_recv(phase, direction):
        for k in ORDER:
            step = -direction * OFFSETS[k][0]
            when_band(step, lambda: route_copy(phase, k, direction).wait_recv())

            def clear():
                brecv[phase, k] = jnp.zeros((cap, width), BF16)

            no_band(step, clear)

    def route_sent(phase, direction):
        for k in ORDER:
            when_band(direction * OFFSETS[k][0], lambda: route_copy(phase, k, direction).wait_send())

    def energy_tile(t, acc):
        te = teach_ref[tile(t), :].astype(F32)
        return acc + jnp.sum(area_ref[tile(t), :] * te * te, axis=0, keepdims=True)

    def folded(acc):
        half = acc[:, :128]
        for i in range(1, width // 128):
            half = half + acc[:, i * 128 : (i + 1) * 128]
        return jnp.where(iota((PAD, 128), 0) == 0, half, 0.0)

    ebuf[me] = folded(lax.fori_loop(0, tiles, energy_tile, jnp.zeros((1, width), F32)))
    e_start()

    edges = lg_row.shape[1]
    MT = 64

    def build_mw(t):
        r = pl.ds(pl.multiple_of(t * MT, MT), MT)
        hit = iota((MT, edges), 0) + t * MT == lm_row[...]
        mw[r, :] = jnp.where(hit, lw_row[...], 0.0).astype(BF16)
        hit = iota((MT, NB * cap), 0) + t * MT == rr_row[...]
        rm[r, :] = jnp.where(hit, rw_row[...], 0.0).astype(BF16)

    loop(mrows // MT, build_mw)

    def build_tile(t):
        gt[...] = jnp.where(iota((TILE, edges), 0) + t * TILE == lg_row[...], 1.0, 0.0).astype(BF16)
        am[:, tile(t)] = nt(mw[...], gt[...]).astype(BF16)
        amt[tile(t), :] = nt(gt[...], mw[...]).astype(BF16)
        hit = iota((TILE, NB * cap), 0) + t * TILE == sr_row[...]
        smt[tile(t), :] = jnp.where(hit, 1.0, 0.0).astype(BF16)

    loop(tiles, build_tile)

    def build_send(k):
        r = pl.ds(pl.multiple_of(k * cap, cap), cap)
        sm[r, :] = jnp.where(iota((cap, rows), 1) == sr_col[r, :], 1.0, 0.0).astype(BF16)
        rmt[r, :] = jnp.where(iota((cap, mrows), 1) == rr_col[r, :], 1.0, 0.0).astype(BF16)

    loop(NB, build_send)
    cn = cm.shape[1]
    cmat = jnp.zeros((mrows, cn), F32)
    cmat_t = jnp.zeros((cn, mrows), F32)
    for k in range(ci_row.shape[0]):
        cmat += jnp.where(iota((mrows, cn), 1) == ci_col[:, k : k + 1], cw_col[:, k : k + 1], 0.0)
        cmat_t += jnp.where(iota((cn, mrows), 0) == ci_row[k : k + 1, :], cw_row[k : k + 1, :], 0.0)
    cm[...] = cmat.astype(BF16)
    cmt[...] = cmat_t.astype(BF16)

    def encode(t):
        x_copy(t).wait_recv()
        pre = nn(grid_ref[tile(t), :], encw_ref[own, :]) + nn(xo[tile(t), :], encw_ref[oth, :])
        pre_enc[tile(t), :] = pre
        enc[tile(t), :] = silu(pre).astype(BF16)

    loop(tiles, encode)

    def to_mesh(values, phase):
        for k in ORDER:
            bsend[phase, k] = nn(sm[k * cap : (k + 1) * cap, :], values[...]).astype(BF16)
            route_start(phase, k, 1)
        total = nn(am[...], values[...])
        bp[...] = total
        route_recv(phase, 1)
        total = bp[...]
        for k in range(NB):
            total += nn(rm[:, k * cap : (k + 1) * cap], brecv[phase, k])
        return total

    def send_messages(values, phase):
        for k in ORDER:
            r = slice(k * cap, (k + 1) * cap)
            bsend[phase, k] = (rw_col[r, :] * nn(rmt[r, :], values)).astype(BF16)
            route_start(phase, k, -1)

    def grid_sum(t, phase):
        total = None
        for k in range(NB):
            part = nn(smt[tile(t), k * cap : (k + 1) * cap], brecv[phase, k])
            total = part if total is None else total + part
        return total

    def exchanged(value, ref, other, i):
        ref[...] = value
        c = partner(ref, other, i)
        c.start()
        return c

    state_f = (init_ref[...].astype(F32) + to_mesh(enc, 0)).astype(BF16)
    c_state = exchanged(state_f, state, stateo, base + 3)
    part = nn(state[...], procw_ref[own, :])
    c_state.wait_recv()
    pre_proc[...] = part + nn(stateo[...], procw_ref[oth, :])
    proc_v[...] = silu(pre_proc[...]).astype(BF16).astype(F32)
    cbuf[sid] = proc_v[0:PAD, :]
    c_start()
    c_recv()
    linked = cbuf[...].reshape(shards * PAD, width).astype(BF16)
    updated = (state[...].astype(F32) + proc_v[...] + nn(cm[...], linked)).astype(BF16)
    c_upd = exchanged(updated, upd, updo, base + 4)
    part = nn(upd[...], decw_ref[own, :])
    c_upd.wait_recv()
    pre_dec[...] = part + nn(updo[...], decw_ref[oth, :])
    decoded = silu(pre_dec[...]).astype(BF16)
    gpp[...] = decoded
    send_messages(gpp[...], 1)

    def local_student(t):
        slope[tile(t), :] = grid_ref[tile(t), :].astype(F32) + nn(amt[tile(t), :], gpp[...])

    loop(tiles, local_student)
    e_recv()
    inv_energy = 1.0 / jnp.sum(jnp.sum(ebuf[...], axis=0), keepdims=True)
    route_recv(1, -1)

    def slope_tile(t, acc):
        student = slope[tile(t), :] + grid_sum(t, 1)
        residual = student - teach_ref[tile(t), :].astype(F32)
        weighted = area_ref[tile(t), :] * residual
        grad = 2.0 * weighted * inv_energy
        slope[tile(t), :] = grad
        slope_half[tile(t), :] = grad.astype(BF16)
        return acc + jnp.sum(weighted * residual, axis=0, keepdims=True)

    acc = lax.fori_loop(0, tiles, slope_tile, jnp.zeros((1, width), F32))
    mbuf[me] = folded(acc)

    back_decoded = to_mesh(slope_half, 2)
    c_gpd = exchanged((back_decoded * silu_slope(pre_dec[...])).astype(BF16), gpd, gpdo, base + 5)
    for c in w_copies:
        c.wait_recv()
    part = nt(gpd[...], decw_ref[own, :])
    c_gpd.wait_recv()
    bu[...] = part + nt(gpdo[...], deco[...])
    tbuf[...] = nn(cmt[...], bu[...].astype(BF16)).reshape(shards, PAD, width)
    rbuf[sid] = tbuf[sid]
    t_start()

    pg[own, :] = tn(upd[...], gpd[...])
    pg[oth, :] = tn(updo[...], gpd[...])
    t_recv()
    if scatter_here:
        share = pg.shape[0] // shards
        g_start, g_recv, g_sent = spread(
            lambda i: pg.at[pl.ds(pl.multiple_of(i * share, PAD), share)], gbuf, gsend, grecv, shards, True
        )
        gbuf[sid] = pg[pl.ds(pl.multiple_of(sid * share, PAD), share), :]

    bp[...] = bu[...]
    bp[0:PAD, :] = bu[0:PAD, :] + jnp.sum(rbuf[...], axis=0)
    c_gpp = exchanged((bp[...] * silu_slope(pre_proc[...])).astype(BF16), gpp, gppo, base + 6)
    part = bu[...] + nt(gpp[...], procw_ref[own, :])
    c_gpp.wait_recv()
    back_mesh = (part + nt(gppo[...], proco[...])).astype(BF16)
    stateo[...] = back_mesh
    send_messages(stateo[...], 3)
    if scatter_here:
        g_start()
    m_start()

    def local_back(t):
        back[tile(t), :] = nn(amt[tile(t), :], stateo[...])
        pre_enc[tile(t), :] = silu_slope(pre_enc[tile(t), :])

    loop(tiles, local_back)
    route_recv(3, -1)

    def back_tile(t):
        total = back[tile(t), :] + grid_sum(t, 3)
        gpe[tile(t), :] = (total * pre_enc[tile(t), :]).astype(BF16)
        g_copy(t).start()

    loop(tiles, back_tile)

    def grad_tile(t):
        part = slope[tile(t), :] + nt(gpe[tile(t), :], encw_ref[own, :])
        g_copy(t).wait_recv()
        gx_ref[tile(t), :] = (part + nt(gpeo[tile(t), :], enco[...])).astype(BF16)

    loop(tiles, grad_tile)
    m_recv()
    misfit = jnp.sum(jnp.sum(mbuf[...], axis=0), keepdims=True)
    loss_ref[...] = jnp.broadcast_to(misfit * inv_energy, loss_ref.shape)
    if scatter_here:
        g_recv()
        gd_ref[...] = jnp.sum(gbuf[...], axis=0)
        g_sent()
    else:
        gd_ref[...] = pg[...]

    def x_sent(t):
        x_copy(t).wait_send()
        g_copy(t).wait_send()

    loop(tiles, x_sent)
    for c in w_copies + [c_state, c_upd, c_gpd, c_gpp]:
        c.wait_send()
    route_sent(0, 1)
    route_sent(1, -1)
    route_sent(2, 1)
    route_sent(3, -1)
    for done in (e_sent, m_sent, c_sent, t_sent):
        done()


def on_device(
    nlat, nlon,
    grid_latent, teacher, mesh_init, enc_weight, proc_weight, dec_weight,
    local_grid, local_mesh, local_weight, send_row, send_count, recv_row, recv_weight,
    coarse_index, coarse_weight,
):
    rows, width = grid_latent.shape
    mrows = mesh_init.shape[0]
    full = enc_weight.shape[0]
    cap = send_row.shape[1]
    edges = local_grid.shape[0]
    shards = nlat * nlon
    nd = 2 * shards
    tiles = rows // TILE
    share = full // shards
    scatter_here = share % PAD == 0
    slots = NB * cap

    slot_ids = jnp.arange(cap, dtype=jnp.int32)
    live = slot_ids[None, :] < send_count[:, None]
    send = jnp.where(live, send_row, -1)
    coarse = (coarse_index // CDEV) * PAD + coarse_index % CDEV
    global_row = lax.axis_index(("lat", "lon")) * rows + jnp.arange(rows, dtype=jnp.int32)
    area = 0.25 + jnp.sin(jnp.pi * (global_row.astype(F32) + 0.5) / (rows * shards))

    operands = (
        grid_latent, teacher, mesh_init, enc_weight, proc_weight, dec_weight, area.reshape(rows, 1),
        local_grid.reshape(1, edges), local_mesh.reshape(1, edges), local_weight.reshape(1, edges),
        send.reshape(1, slots), send.reshape(slots, 1),
        recv_row.reshape(1, slots), recv_row.reshape(slots, 1),
        recv_weight.reshape(1, slots), recv_weight.reshape(slots, 1),
        coarse, coarse.T, coarse_weight, coarse_weight.T,
    )
    dma = pltpu.SemaphoreType.DMA
    V = pltpu.VMEM
    big = (rows, width)
    mid = (mrows, width)
    scratch = [
        V(big, BF16), V((width, width), BF16), V((width, width), BF16), V((width, width), BF16),
        V((mrows, edges), BF16), V((TILE, edges), BF16), V((mrows, rows), BF16), V((rows, mrows), BF16),
        V((slots, rows), BF16), V((rows, slots), BF16), V((mrows, slots), BF16), V((slots, mrows), BF16),
        V((mrows, PAD * shards), BF16), V((PAD * shards, mrows), BF16),
        V(big, F32), V(big, BF16), V(big, F32), V(big, BF16), V(big, BF16), V(big, BF16), V(big, F32),
        V((4, NB, cap, width), BF16), V((4, NB, cap, width), BF16),
        V(mid, BF16), V(mid, BF16), V(mid, F32), V(mid, F32), V(mid, BF16), V(mid, BF16), V(mid, F32),
        V(mid, BF16), V(mid, BF16), V(mid, F32), V(mid, F32), V(mid, BF16), V(mid, BF16),
        V((nd, PAD, 128), F32), V((nd, PAD, 128), F32), V((shards, PAD, width), F32),
        V((shards, PAD, width), F32), V((shards, PAD, width), F32),
        V((full, width), F32), V((shards, max(share, PAD), width), F32),
        dma((2 * tiles + 7,)), dma((2 * tiles + 7,)), dma((4, NB)), dma((4, NB)),
        dma((nd,)), dma((nd,)), dma((nd,)), dma((nd,)),
        dma((shards,)), dma((shards,)), dma((shards,)), dma((shards,)), dma((shards,)), dma((shards,)),
    ]
    vmem = pl.BlockSpec(memory_space=pltpu.VMEM)
    loss, grad_x, grad_dec = pl.pallas_call(
        functools.partial(kernel, nlat, nlon, scatter_here),
        out_shape=(
            jax.ShapeDtypeStruct((PAD, 128), F32),
            jax.ShapeDtypeStruct(big, BF16),
            jax.ShapeDtypeStruct((share if scatter_here else full, width), F32),
        ),
        in_specs=[vmem] * len(operands),
        out_specs=(vmem,) * 3,
        scratch_shapes=scratch,
        compiler_params=pltpu.CompilerParams(
            collective_id=0, has_side_effects=True, vmem_limit_bytes=58 * 2**20
        ),
    )(*operands)
    if not scatter_here:
        grad_dec = lax.psum_scatter(grad_dec, ("lat", "lon"), scatter_dimension=0, tiled=True)
    return (loss[0, :1], grad_x, grad_dec)


def solution(mesh):
    rows = P(("groups", "lat", "lon"), "feat")
    cols = P(None, "feat")
    flat = P(("lat", "lon"))
    table = P(("lat", "lon"), None)
    return jax.shard_map(
        functools.partial(on_device, mesh.shape["lat"], mesh.shape["lon"]),
        mesh=mesh,
        in_specs=(rows,) * 3 + (cols,) * 3 + (flat,) * 3 + (table, flat, table, table, table, table),
        out_specs=(P("groups"), rows, rows),
        check_vma=False,
    )
```

```python
import functools

import jax
import jax.numpy as jnp
from jax import lax
from jax.experimental import pallas as pl
from jax.experimental.pallas import tpu as pltpu
from jax.sharding import PartitionSpec as P

CDEV = 4
PAD = 8
TILE = 256
OFFSETS = ((-1, 0), (1, 0), (-1, 1), (0, 1), (1, 1))
NB = len(OFFSETS)
MESH_ID = pl.DeviceIdType.MESH
F32 = jnp.float32
BF16 = jnp.bfloat16


def silu(v):
    return v * jax.nn.sigmoid(v)


def silu_slope(v):
    q = jax.nn.sigmoid(v)
    return q * (1.0 + v * (1.0 - q))


def nn(a, b):
    return jnp.dot(a, b, preferred_element_type=F32)


def nt(a, b):
    return lax.dot_general(a, b, (((1,), (1,)), ((), ())), preferred_element_type=F32)


def tn(a, b):
    return lax.dot_general(a, b, (((0,), (0,)), ((), ())), preferred_element_type=F32)


def iota(shape, dim):
    return lax.broadcasted_iota(jnp.int32, shape, dim)


def kernel(
    nlat, nlon, scatter_here,
    grid_ref, teach_ref, init_ref, encw_ref, procw_ref, decw_ref,
    lg_row, lm_row, lw_row, sr, rr, rw, ci_row, cw_row,
    loss_ref, gx_ref, gd_ref,
    xo, enco, proco, deco,
    mw, gt, am, amt, sm, smt, rm, rmt, cmt, area_ref, rw_col,
    pre_enc, enc, slope, slope_half, gpe, gpeo, back,
    bsend, brecv,
    state, stateo, pre_proc, proc_v, upd, updo, pre_dec, gpd, gpdo, bu, bp, gpp, gppo,
    ebuf, mbuf, cbuf, tbuf, rbuf, pg, gbuf,
    psend, precv, rsend, rrecv, esend, erecv, msend, mrecv, csend, crecv, tsend, trecv, gsend, grecv,
):
    b = lax.axis_index("lat")
    o = lax.axis_index("lon")
    f = lax.axis_index("feat")
    nd = nlat * nlon * 2
    shards = nlat * nlon
    sid = b * nlon + o
    me = sid * 2 + f
    rows, width = grid_ref.shape
    mrows = init_ref.shape[0]
    cap = rr.shape[1]
    tiles = rows // TILE
    own = pl.ds(pl.multiple_of(f * width, width), width)
    oth = pl.ds(pl.multiple_of((1 - f) * width, width), width)

    def tile(t):
        return pl.ds(pl.multiple_of(t * TILE, TILE), TILE)

    def column(row):
        n = row.shape[1]
        return jnp.sum(jnp.where(iota((n, n), 0) == iota((n, n), 1), row, 0.0), axis=1, keepdims=True)

    def int_column(row):
        return column(row.astype(F32)).astype(jnp.int32)

    def loop(n, body, start=0):
        lax.fori_loop(start, n, lambda i, c: (body(i), c)[1], 0)

    barrier = pltpu.get_barrier_semaphore()

    def greet(r):
        d = lax.rem(me + r, nd)
        pl.semaphore_signal(
            barrier, inc=1, device_id_type=MESH_ID,
            device_id={"lat": d // (2 * nlon), "lon": lax.rem(d // 2, nlon), "feat": lax.rem(d, 2)},
        )

    loop(nd, greet, 1)
    pl.semaphore_wait(barrier, nd - 1)

    def partner(src, dst, i):
        return pltpu.make_async_remote_copy(
            src_ref=src, dst_ref=dst, send_sem=psend.at[i], recv_sem=precv.at[i],
            device_id={"feat": 1 - f}, device_id_type=MESH_ID,
        )

    def x_copy(t):
        return partner(grid_ref.at[tile(t)], xo.at[tile(t)], t)

    def g_copy(t):
        return partner(gpe.at[tile(t)], gpeo.at[tile(t)], tiles + t)

    base = 2 * tiles
    w_copies = [
        partner(decw_ref.at[oth], deco, base),
        partner(procw_ref.at[oth], proco, base + 1),
        partner(encw_ref.at[oth], enco, base + 2),
    ]
    loop(tiles, lambda t: x_copy(t).start())
    for c in w_copies:
        c.start()

    def spread(buf_from, buf_to, ss, rs, count, scatter):
        whole_group = count == nd
        mine = me if whole_group else sid

        def copy(r):
            d = lax.rem(mine + r, count)
            src = buf_from(d) if scatter else buf_from(mine)
            if whole_group:
                where = {"lat": d // (2 * nlon), "lon": lax.rem(d // 2, nlon), "feat": lax.rem(d, 2)}
            else:
                where = {"lat": d // nlon, "lon": lax.rem(d, nlon)}
            return pltpu.make_async_remote_copy(
                src_ref=src, dst_ref=buf_to.at[mine], send_sem=ss.at[d], recv_sem=rs.at[mine],
                device_id=where, device_id_type=MESH_ID,
            )

        def arrival(r):
            d = lax.rem(mine + r, count)
            return pltpu.make_async_remote_copy(
                src_ref=buf_to.at[d], dst_ref=buf_to.at[d], send_sem=ss.at[d], recv_sem=rs.at[d],
                device_id={"feat": 1 - f}, device_id_type=MESH_ID,
            )

        return (
            lambda: loop(count, lambda r: copy(r).start(), 1),
            lambda: loop(count, lambda r: arrival(r).wait_recv(), 1),
            lambda: loop(count, lambda r: copy(r).wait_send(), 1),
        )

    e_start, e_recv, e_sent = spread(lambda i: ebuf.at[i], ebuf, esend, erecv, nd, False)
    m_start, m_recv, m_sent = spread(lambda i: mbuf.at[i], mbuf, msend, mrecv, nd, False)
    c_start, c_recv, c_sent = spread(lambda i: cbuf.at[i], cbuf, csend, crecv, shards, False)
    t_start, t_recv, t_sent = spread(lambda i: tbuf.at[i], rbuf, tsend, trecv, shards, True)

    def route_copy(phase, k, direction):
        db, do = OFFSETS[k]
        return pltpu.make_async_remote_copy(
            src_ref=bsend.at[phase, k], dst_ref=brecv.at[phase, k],
            send_sem=rsend.at[phase, k], recv_sem=rrecv.at[phase, k],
            device_id={"lat": b + direction * db, "lon": lax.rem(o + direction * do + nlon, nlon)},
            device_id_type=MESH_ID,
        )

    def when_band(step, fn):
        if step == 0:
            fn()
        elif step > 0:
            pl.when(b < nlat - 1)(fn)
        else:
            pl.when(b > 0)(fn)

    def no_band(step, fn):
        if step > 0:
            pl.when(b == nlat - 1)(fn)
        elif step < 0:
            pl.when(b == 0)(fn)

    ORDER = (2, 4, 3, 0, 1)

    def route_start(phase, k, direction):
        when_band(direction * OFFSETS[k][0], lambda: route_copy(phase, k, direction).start())

    def route_recv(phase, direction):
        for k in ORDER:
            step = -direction * OFFSETS[k][0]
            when_band(step, lambda: route_copy(phase, k, direction).wait_recv())

            def clear():
                brecv[phase, k] = jnp.zeros((cap, width), BF16)

            no_band(step, clear)

    def route_sent(phase, direction):
        for k in ORDER:
            when_band(direction * OFFSETS[k][0], lambda: route_copy(phase, k, direction).wait_send())

    total_rows = rows * shards

    def energy_tile(t, acc):
        g = (sid * rows + t * TILE + iota((PAD, TILE), 1)).astype(F32)
        area = 0.25 + jnp.sin(jnp.pi * (g + 0.5) / total_rows)
        area_ref[tile(t), :] = column(area[0:1, :])
        te = teach_ref[tile(t), :].astype(F32)
        return acc + jnp.sum(area_ref[tile(t), :] * te * te, axis=0, keepdims=True)

    def folded(acc):
        half = acc[:, :128]
        for i in range(1, width // 128):
            half = half + acc[:, i * 128 : (i + 1) * 128]
        return jnp.where(iota((PAD, 128), 0) == 0, half, 0.0)

    ebuf[me] = folded(lax.fori_loop(0, tiles, energy_tile, jnp.zeros((1, width), F32)))
    e_start()

    edges = lg_row.shape[1]
    MT = 64

    for k in range(NB):
        hit = iota((cap, rows), 1) == int_column(sr[k : k + 1, :])
        sm[k * cap : (k + 1) * cap, :] = jnp.where(hit, 1.0, 0.0).astype(BF16)

    def build_mw(t):
        r = pl.ds(pl.multiple_of(t * MT, MT), MT)
        hit = iota((MT, edges), 0) + t * MT == lm_row[...]
        mw[r, :] = jnp.where(hit, lw_row[...], 0.0).astype(BF16)
        for k in range(NB):
            hit = iota((MT, cap), 0) + t * MT == rr[k : k + 1, :]
            rm[r, k * cap : (k + 1) * cap] = jnp.where(hit, rw[k : k + 1, :], 0.0).astype(BF16)

    def build_tile(t):
        gt[...] = jnp.where(iota((TILE, edges), 0) + t * TILE == lg_row[...], 1.0, 0.0).astype(BF16)
        am[:, tile(t)] = nt(mw[...], gt[...]).astype(BF16)
        amt[tile(t), :] = nt(gt[...], mw[...]).astype(BF16)
        for k in range(NB):
            hit = iota((TILE, cap), 0) + t * TILE == sr[k : k + 1, :]
            smt[tile(t), k * cap : (k + 1) * cap] = jnp.where(hit, 1.0, 0.0).astype(BF16)

    def build_tables():
        loop(mrows // MT, build_mw)
        loop(tiles, build_tile)
        for k in range(NB):
            r = slice(k * cap, (k + 1) * cap)
            hit = iota((cap, mrows), 1) == int_column(rr[k : k + 1, :])
            rmt[r, :] = jnp.where(hit, 1.0, 0.0).astype(BF16)
            rw_col[r, :] = column(rw[k : k + 1, :])
        cn = cmt.shape[0]
        cmat_t = jnp.zeros((cn, mrows), F32)
        for k in range(ci_row.shape[0]):
            j = ci_row[k : k + 1, :]
            j = (j // CDEV) * PAD + lax.rem(j, CDEV)
            cmat_t += jnp.where(iota((cn, mrows), 0) == j, cw_row[k : k + 1, :], 0.0)
        cmt[...] = cmat_t.astype(BF16)

    def encode(t):
        x_copy(t).wait_recv()
        pre = nn(grid_ref[tile(t), :], encw_ref[own, :]) + nn(xo[tile(t), :], encw_ref[oth, :])
        pre_enc[tile(t), :] = pre
        enc[tile(t), :] = silu(pre).astype(BF16)

    loop(tiles, encode)

    def to_mesh(values, phase):
        for k in ORDER:
            bsend[phase, k] = nn(sm[k * cap : (k + 1) * cap, :], values[...]).astype(BF16)
            route_start(phase, k, 1)
        if phase == 0:
            build_tables()
        total = nn(am[...], values[...])
        bp[...] = total
        route_recv(phase, 1)
        total = bp[...]
        for k in range(NB):
            total += nn(rm[:, k * cap : (k + 1) * cap], brecv[phase, k])
        return total

    def send_messages(values, phase):
        for k in ORDER:
            r = slice(k * cap, (k + 1) * cap)
            bsend[phase, k] = (rw_col[r, :] * nn(rmt[r, :], values)).astype(BF16)
            route_start(phase, k, -1)

    def grid_sum(t, phase):
        total = None
        for k in range(NB):
            part = nn(smt[tile(t), k * cap : (k + 1) * cap], brecv[phase, k])
            total = part if total is None else total + part
        return total

    def exchanged(value, ref, other, i):
        ref[...] = value
        c = partner(ref, other, i)
        c.start()
        return c

    state_f = (init_ref[...].astype(F32) + to_mesh(enc, 0)).astype(BF16)
    c_state = exchanged(state_f, state, stateo, base + 3)
    part = nn(state[...], procw_ref[own, :])
    c_state.wait_recv()
    pre_proc[...] = part + nn(stateo[...], procw_ref[oth, :])
    proc_v[...] = silu(pre_proc[...]).astype(BF16).astype(F32)
    cbuf[sid] = proc_v[0:PAD, :]
    c_start()
    c_recv()
    linked = cbuf[...].reshape(shards * PAD, width).astype(BF16)
    updated = (state[...].astype(F32) + proc_v[...] + tn(cmt[...], linked)).astype(BF16)
    c_upd = exchanged(updated, upd, updo, base + 4)
    part = nn(upd[...], decw_ref[own, :])
    c_upd.wait_recv()
    pre_dec[...] = part + nn(updo[...], decw_ref[oth, :])
    decoded = silu(pre_dec[...]).astype(BF16)
    gpp[...] = decoded
    send_messages(gpp[...], 1)

    def local_student(t):
        slope[tile(t), :] = grid_ref[tile(t), :].astype(F32) + nn(amt[tile(t), :], gpp[...])

    loop(tiles, local_student)
    e_recv()
    inv_energy = 1.0 / jnp.sum(jnp.sum(ebuf[...], axis=0), keepdims=True)
    route_recv(1, -1)

    def slope_tile(t, acc):
        student = slope[tile(t), :] + grid_sum(t, 1)
        residual = student - teach_ref[tile(t), :].astype(F32)
        weighted = area_ref[tile(t), :] * residual
        grad = 2.0 * weighted * inv_energy
        slope[tile(t), :] = grad
        slope_half[tile(t), :] = grad.astype(BF16)
        return acc + jnp.sum(weighted * residual, axis=0, keepdims=True)

    acc = lax.fori_loop(0, tiles, slope_tile, jnp.zeros((1, width), F32))
    mbuf[me] = folded(acc)

    back_decoded = to_mesh(slope_half, 2)
    c_gpd = exchanged((back_decoded * silu_slope(pre_dec[...])).astype(BF16), gpd, gpdo, base + 5)
    for c in w_copies:
        c.wait_recv()
    part = nt(gpd[...], decw_ref[own, :])
    c_gpd.wait_recv()
    bu[...] = part + nt(gpdo[...], deco[...])
    tbuf[...] = nn(cmt[...], bu[...].astype(BF16)).reshape(shards, PAD, width)
    rbuf[sid] = tbuf[sid]
    t_start()

    pg[own, :] = tn(upd[...], gpd[...]).astype(pg.dtype)
    pg[oth, :] = tn(updo[...], gpd[...]).astype(pg.dtype)
    if scatter_here:
        share = pg.shape[0] // shards
        g_start, g_recv, g_sent = spread(
            lambda i: pg.at[pl.ds(pl.multiple_of(i * share, 2 * PAD), share)], gbuf, gsend, grecv, shards, True
        )
        g_start()
        gbuf[sid] = pg[pl.ds(pl.multiple_of(sid * share, 2 * PAD), share), :]
    t_recv()

    bp[...] = bu[...]
    bp[0:PAD, :] = bu[0:PAD, :] + jnp.sum(rbuf[...], axis=0)
    c_gpp = exchanged((bp[...] * silu_slope(pre_proc[...])).astype(BF16), gpp, gppo, base + 6)
    part = bu[...] + nt(gpp[...], procw_ref[own, :])
    c_gpp.wait_recv()
    back_mesh = (part + nt(gppo[...], proco[...])).astype(BF16)
    stateo[...] = back_mesh
    send_messages(stateo[...], 3)
    m_start()

    def local_back(t):
        back[tile(t), :] = nn(amt[tile(t), :], stateo[...])
        pre_enc[tile(t), :] = silu_slope(pre_enc[tile(t), :])

    loop(tiles, local_back)
    route_recv(3, -1)

    def back_tile(t):
        total = back[tile(t), :] + grid_sum(t, 3)
        gpe[tile(t), :] = (total * pre_enc[tile(t), :]).astype(BF16)
        g_copy(t).start()

    loop(tiles, back_tile)

    def grad_tile(t):
        part = slope[tile(t), :] + nt(gpe[tile(t), :], encw_ref[own, :])
        g_copy(t).wait_recv()
        gx_ref[tile(t), :] = (part + nt(gpeo[tile(t), :], enco[...])).astype(BF16)

    loop(tiles, grad_tile)
    m_recv()
    misfit = jnp.sum(jnp.sum(mbuf[...], axis=0), keepdims=True)
    loss_ref[0] = jnp.sum(misfit * inv_energy)
    if scatter_here:
        g_recv()
        gd_ref[...] = jnp.sum(gbuf[...].astype(F32), axis=0)
        g_sent()
    else:
        gd_ref[...] = pg[...]

    def x_sent(t):
        x_copy(t).wait_send()
        g_copy(t).wait_send()

    loop(tiles, x_sent)
    for c in w_copies + [c_state, c_upd, c_gpd, c_gpp]:
        c.wait_send()
    route_sent(0, 1)
    route_sent(1, -1)
    route_sent(2, 1)
    route_sent(3, -1)
    for done in (e_sent, m_sent, c_sent, t_sent):
        done()


def on_device(
    nlat, nlon,
    grid_latent, teacher, mesh_init, enc_weight, proc_weight, dec_weight,
    local_grid, local_mesh, local_weight, send_row, send_count, recv_row, recv_weight,
    coarse_index, coarse_weight,
):
    rows, width = grid_latent.shape
    mrows = mesh_init.shape[0]
    full = enc_weight.shape[0]
    cap = send_row.shape[1]
    edges = local_grid.shape[0]
    shards = nlat * nlon
    nd = 2 * shards
    tiles = rows // TILE
    share = full // shards
    scatter_here = share % (2 * PAD) == 0
    slots = NB * cap

    slot_ids = jnp.arange(cap, dtype=jnp.int32)
    live = slot_ids[None, :] < send_count[:, None]
    send = jnp.where(live, send_row, -1)
    operands = (
        grid_latent, teacher, mesh_init, enc_weight, proc_weight, dec_weight,
        local_grid.reshape(1, edges), local_mesh.reshape(1, edges), local_weight.reshape(1, edges),
        send, recv_row, recv_weight, coarse_index.T, coarse_weight.T,
    )
    dma = pltpu.SemaphoreType.DMA
    V = pltpu.VMEM
    big = (rows, width)
    mid = (mrows, width)
    scratch = [
        V(big, BF16), V((width, width), BF16), V((width, width), BF16), V((width, width), BF16),
        V((mrows, edges), BF16), V((TILE, edges), BF16), V((mrows, rows), BF16), V((rows, mrows), BF16),
        V((slots, rows), BF16), V((rows, slots), BF16), V((mrows, slots), BF16), V((slots, mrows), BF16),
        V((PAD * shards, mrows), BF16), V((rows, 1), F32), V((slots, 1), F32),
        V(big, F32), V(big, BF16), V(big, F32), V(big, BF16), V(big, BF16), V(big, BF16), V(big, F32),
        V((4, NB, cap, width), BF16), V((4, NB, cap, width), BF16),
        V(mid, BF16), V(mid, BF16), V(mid, F32), V(mid, F32), V(mid, BF16), V(mid, BF16), V(mid, F32),
        V(mid, BF16), V(mid, BF16), V(mid, F32), V(mid, F32), V(mid, BF16), V(mid, BF16),
        V((nd, PAD, 128), F32), V((nd, PAD, 128), F32), V((shards, PAD, width), F32),
        V((shards, PAD, width), F32), V((shards, PAD, width), F32),
        V((full, width), BF16 if scatter_here else F32), V((shards, max(share, 2 * PAD), width), BF16),
        dma((2 * tiles + 7,)), dma((2 * tiles + 7,)), dma((4, NB)), dma((4, NB)),
        dma((nd,)), dma((nd,)), dma((nd,)), dma((nd,)),
        dma((shards,)), dma((shards,)), dma((shards,)), dma((shards,)), dma((shards,)), dma((shards,)),
    ]
    vmem = pl.BlockSpec(memory_space=pltpu.VMEM)
    loss, grad_x, grad_dec = pl.pallas_call(
        functools.partial(kernel, nlat, nlon, scatter_here),
        out_shape=(
            jax.ShapeDtypeStruct((1,), F32),
            jax.ShapeDtypeStruct(big, BF16),
            jax.ShapeDtypeStruct((share if scatter_here else full, width), F32),
        ),
        in_specs=[vmem] * len(operands),
        out_specs=(pl.BlockSpec(memory_space=pltpu.SMEM), vmem, vmem),
        scratch_shapes=scratch,
        compiler_params=pltpu.CompilerParams(
            collective_id=0, has_side_effects=True, vmem_limit_bytes=58 * 2**20
        ),
    )(*operands)
    if not scatter_here:
        grad_dec = lax.psum_scatter(grad_dec, ("lat", "lon"), scatter_dimension=0, tiled=True)
    return (loss, grad_x, grad_dec)


def solution(mesh):
    rows = P(("groups", "lat", "lon"), "feat")
    cols = P(None, "feat")
    flat = P(("lat", "lon"))
    table = P(("lat", "lon"), None)
    return jax.shard_map(
        functools.partial(on_device, mesh.shape["lat"], mesh.shape["lon"]),
        mesh=mesh,
        in_specs=(rows,) * 3 + (cols,) * 3 + (flat,) * 3 + (table, flat, table, table, table, table),
        out_specs=(P("groups"), rows, rows),
        check_vma=False,
    )
```

```python
import functools

import jax
import jax.numpy as jnp
from jax import lax
from jax.experimental import pallas as pl
from jax.experimental.pallas import tpu as pltpu
from jax.sharding import PartitionSpec as P

CDEV = 4
PAD = 8
TILE = 256
OFFSETS = ((-1, 0), (1, 0), (-1, 1), (0, 1), (1, 1))
NB = len(OFFSETS)
MESH_ID = pl.DeviceIdType.MESH
F32 = jnp.float32
BF16 = jnp.bfloat16


def silu(v):
    return v * jax.nn.sigmoid(v)


def silu_slope(v):
    q = jax.nn.sigmoid(v)
    return q * (1.0 + v * (1.0 - q))


def nn(a, b):
    return jnp.dot(a, b, preferred_element_type=F32)


def nt(a, b):
    return lax.dot_general(a, b, (((1,), (1,)), ((), ())), preferred_element_type=F32)


def tn(a, b):
    return lax.dot_general(a, b, (((0,), (0,)), ((), ())), preferred_element_type=F32)


def iota(shape, dim):
    return lax.broadcasted_iota(jnp.int32, shape, dim)


def kernel(
    nlat, nlon, scatter_here,
    grid_ref, teach_ref, init_ref, encw_ref, procw_ref, decw_ref,
    lg_row, lm_row, lw_row, sr, rr, rw, ci_row, cw_row,
    loss_ref, gx_ref, gd_ref,
    xo, enco, proco, deco,
    mw, gt, am, amt, sm, smt, rm, rmt, cmt, area_ref, rw_col,
    pre_enc, enc, slope, slope_half, gpe, gpeo, back,
    bsend, brecv,
    state, stateo, pre_proc, proc_v, upd, updo, pre_dec, gpd, gpdo, bu, bp, gpp, gppo,
    ebuf, mbuf, cbuf, tbuf, rbuf, pg, gbuf,
    psend, precv, rsend, rrecv, esend, erecv, msend, mrecv, csend, crecv, tsend, trecv, gsend, grecv,
):
    b = lax.axis_index("lat")
    o = lax.axis_index("lon")
    f = lax.axis_index("feat")
    nd = nlat * nlon * 2
    shards = nlat * nlon
    sid = b * nlon + o
    me = sid * 2 + f
    rows, width = grid_ref.shape
    mrows = init_ref.shape[0]
    cap = rr.shape[1]
    tiles = rows // TILE
    own = pl.ds(pl.multiple_of(f * width, width), width)
    oth = pl.ds(pl.multiple_of((1 - f) * width, width), width)

    def tile(t):
        return pl.ds(pl.multiple_of(t * TILE, TILE), TILE)

    def column(row):
        n = row.shape[1]
        return jnp.sum(jnp.where(iota((n, n), 0) == iota((n, n), 1), row, 0.0), axis=1, keepdims=True)

    def int_column(row):
        return column(row.astype(F32)).astype(jnp.int32)

    def loop(n, body, start=0):
        lax.fori_loop(start, n, lambda i, c: (body(i), c)[1], 0)

    barrier = pltpu.get_barrier_semaphore()

    def greet(r):
        d = lax.rem(me + r, nd)
        pl.semaphore_signal(
            barrier, inc=1, device_id_type=MESH_ID,
            device_id={"lat": d // (2 * nlon), "lon": lax.rem(d // 2, nlon), "feat": lax.rem(d, 2)},
        )

    loop(nd, greet, 1)
    for k in range(NB):
        hit = iota((cap, rows), 1) == int_column(sr[k : k + 1, :])
        sm[k * cap : (k + 1) * cap, :] = jnp.where(hit, 1.0, 0.0).astype(BF16)

    pl.semaphore_wait(barrier, nd - 1)

    def partner(src, dst, i):
        return pltpu.make_async_remote_copy(
            src_ref=src, dst_ref=dst, send_sem=psend.at[i], recv_sem=precv.at[i],
            device_id={"feat": 1 - f}, device_id_type=MESH_ID,
        )

    def x_copy(t):
        return partner(grid_ref.at[tile(t)], xo.at[tile(t)], t)

    def g_copy(t):
        return partner(gpe.at[tile(t)], gpeo.at[tile(t)], tiles + t)

    base = 2 * tiles
    w_copies = [
        partner(decw_ref.at[oth], deco, base),
        partner(procw_ref.at[oth], proco, base + 1),
        partner(encw_ref.at[oth], enco, base + 2),
    ]
    loop(tiles, lambda t: x_copy(t).start())
    for c in w_copies:
        c.start()

    def spread(buf_from, buf_to, ss, rs, count, scatter):
        whole_group = count == nd
        mine = me if whole_group else sid

        def copy(r):
            d = lax.rem(mine + r, count)
            src = buf_from(d) if scatter else buf_from(mine)
            if whole_group:
                where = {"lat": d // (2 * nlon), "lon": lax.rem(d // 2, nlon), "feat": lax.rem(d, 2)}
            else:
                where = {"lat": d // nlon, "lon": lax.rem(d, nlon)}
            return pltpu.make_async_remote_copy(
                src_ref=src, dst_ref=buf_to.at[mine], send_sem=ss.at[d], recv_sem=rs.at[mine],
                device_id=where, device_id_type=MESH_ID,
            )

        def arrival(r):
            d = lax.rem(mine + r, count)
            return pltpu.make_async_remote_copy(
                src_ref=buf_to.at[d], dst_ref=buf_to.at[d], send_sem=ss.at[d], recv_sem=rs.at[d],
                device_id={"feat": 1 - f}, device_id_type=MESH_ID,
            )

        return (
            lambda: loop(count, lambda r: copy(r).start(), 1),
            lambda: loop(count, lambda r: arrival(r).wait_recv(), 1),
            lambda: loop(count, lambda r: copy(r).wait_send(), 1),
        )

    e_start, e_recv, e_sent = spread(lambda i: ebuf.at[i], ebuf, esend, erecv, nd, False)
    m_start, m_recv, m_sent = spread(lambda i: mbuf.at[i], mbuf, msend, mrecv, nd, False)
    c_start, c_recv, c_sent = spread(lambda i: cbuf.at[i], cbuf, csend, crecv, shards, False)
    t_start, t_recv, t_sent = spread(lambda i: tbuf.at[i], rbuf, tsend, trecv, shards, True)

    def route_copy(phase, k, direction):
        db, do = OFFSETS[k]
        return pltpu.make_async_remote_copy(
            src_ref=bsend.at[phase, k], dst_ref=brecv.at[phase, pl.ds(k * cap, cap)],
            send_sem=rsend.at[phase, k], recv_sem=rrecv.at[phase, k],
            device_id={"lat": b + direction * db, "lon": lax.rem(o + direction * do + nlon, nlon)},
            device_id_type=MESH_ID,
        )

    def when_band(step, fn):
        if step == 0:
            fn()
        elif step > 0:
            pl.when(b < nlat - 1)(fn)
        else:
            pl.when(b > 0)(fn)

    def no_band(step, fn):
        if step > 0:
            pl.when(b == nlat - 1)(fn)
        elif step < 0:
            pl.when(b == 0)(fn)

    ORDER = (2, 4, 3, 0, 1)

    def route_start(phase, k, direction):
        when_band(direction * OFFSETS[k][0], lambda: route_copy(phase, k, direction).start())

    def route_recv(phase, direction):
        for k in ORDER:
            step = -direction * OFFSETS[k][0]
            when_band(step, lambda: route_copy(phase, k, direction).wait_recv())

            def clear():
                brecv[phase, k * cap : (k + 1) * cap, :] = jnp.zeros((cap, width), BF16)

            no_band(step, clear)

    def route_sent(phase, direction):
        for k in ORDER:
            when_band(direction * OFFSETS[k][0], lambda: route_copy(phase, k, direction).wait_send())

    total_rows = rows * shards

    def energy_tile(t, acc):
        g = (sid * rows + t * TILE + iota((PAD, TILE), 1)).astype(F32)
        area = 0.25 + jnp.sin(jnp.pi * (g + 0.5) / total_rows)
        area_ref[tile(t), :] = column(area[0:1, :])
        te = teach_ref[tile(t), :].astype(F32)
        return acc + jnp.sum(area_ref[tile(t), :] * te * te, axis=0, keepdims=True)

    def folded(acc):
        half = acc[:, :128]
        for i in range(1, width // 128):
            half = half + acc[:, i * 128 : (i + 1) * 128]
        return jnp.where(iota((PAD, 128), 0) == 0, half, 0.0)

    ebuf[me] = folded(lax.fori_loop(0, tiles, energy_tile, jnp.zeros((1, width), F32)))
    e_start()

    edges = lg_row.shape[1]
    MT = 64

    def build_mw(t):
        r = pl.ds(pl.multiple_of(t * MT, MT), MT)
        hit = iota((MT, edges), 0) + t * MT == lm_row[...]
        mw[r, :] = jnp.where(hit, lw_row[...], 0.0).astype(BF16)
        for k in range(NB):
            hit = iota((MT, cap), 0) + t * MT == rr[k : k + 1, :]
            rm[r, k * cap : (k + 1) * cap] = jnp.where(hit, rw[k : k + 1, :], 0.0).astype(BF16)

    def build_tile(t):
        hit = iota((TILE, edges), 0) + t * TILE == lg_row[...]
        gt[tile(t), :] = jnp.where(hit, 1.0, 0.0).astype(BF16)
        am[:, tile(t)] = nt(mw[...], gt[tile(t), :]).astype(BF16)

    def build_back(t):
        amt[tile(t), :] = nt(gt[tile(t), :], mw[...]).astype(BF16)

    def build_arrive(t):
        for k in range(NB):
            hit = iota((TILE, cap), 0) + t * TILE == sr[k : k + 1, :]
            smt[tile(t), k * cap : (k + 1) * cap] = jnp.where(hit, 1.0, 0.0).astype(BF16)

    def build_tables():
        loop(mrows // MT, build_mw)
        loop(tiles, build_tile)
        cn = cmt.shape[0]
        cmat_t = jnp.zeros((cn, mrows), F32)
        for k in range(ci_row.shape[0]):
            j = ci_row[k : k + 1, :]
            j = (j // CDEV) * PAD + lax.rem(j, CDEV)
            cmat_t += jnp.where(iota((cn, mrows), 0) == j, cw_row[k : k + 1, :], 0.0)
        cmt[...] = cmat_t.astype(BF16)

    def build_messages():
        for k in range(NB):
            r = slice(k * cap, (k + 1) * cap)
            hit = iota((cap, mrows), 1) == int_column(rr[k : k + 1, :])
            rmt[r, :] = jnp.where(hit, 1.0, 0.0).astype(BF16)
            rw_col[r, :] = column(rw[k : k + 1, :])
        loop(tiles, build_arrive)

    def encode(t):
        x_copy(t).wait_recv()
        pre = nn(grid_ref[tile(t), :], encw_ref[own, :]) + nn(xo[tile(t), :], encw_ref[oth, :])
        pre_enc[tile(t), :] = pre
        enc[tile(t), :] = silu(pre).astype(BF16)

    loop(tiles, encode)

    def to_mesh(values, phase):
        for k in ORDER:
            bsend[phase, k] = nn(sm[k * cap : (k + 1) * cap, :], values[...]).astype(BF16)
            route_start(phase, k, 1)
        if phase == 0:
            build_tables()
        total = nn(am[...], values[...])
        bp[...] = total
        route_recv(phase, 1)
        return bp[...] + nn(rm[...], brecv[phase])

    def send_messages(values, phase):
        for k in ORDER:
            r = slice(k * cap, (k + 1) * cap)
            bsend[phase, k] = (rw_col[r, :] * nn(rmt[r, :], values)).astype(BF16)
            route_start(phase, k, -1)

    def grid_sum(t, phase):
        return nn(smt[tile(t), :], brecv[phase])

    def exchanged(value, ref, other, i):
        ref[...] = value
        c = partner(ref, other, i)
        c.start()
        return c

    state_f = (init_ref[...].astype(F32) + to_mesh(enc, 0)).astype(BF16)
    c_state = exchanged(state_f, state, stateo, base + 3)
    part = nn(state[...], procw_ref[own, :])
    c_state.wait_recv()
    pre_proc[...] = part + nn(stateo[...], procw_ref[oth, :])
    proc_v[...] = silu(pre_proc[...]).astype(BF16).astype(F32)
    cbuf[sid] = proc_v[0:PAD, :]
    c_start()
    build_messages()
    c_recv()
    linked = cbuf[...].reshape(shards * PAD, width).astype(BF16)
    updated = (state[...].astype(F32) + proc_v[...] + tn(cmt[...], linked)).astype(BF16)
    c_upd = exchanged(updated, upd, updo, base + 4)
    part = nn(upd[...], decw_ref[own, :])
    c_upd.wait_recv()
    pre_dec[...] = part + nn(updo[...], decw_ref[oth, :])
    decoded = silu(pre_dec[...]).astype(BF16)
    gpp[...] = decoded
    send_messages(gpp[...], 1)

    def local_student(t):
        slope[tile(t), :] = grid_ref[tile(t), :].astype(F32) + nn(amt[tile(t), :], gpp[...])

    loop(tiles, build_back)
    loop(tiles, local_student)
    e_recv()
    inv_energy = 1.0 / jnp.sum(jnp.sum(ebuf[...], axis=0), keepdims=True)
    route_recv(1, -1)

    def slope_tile(t, acc):
        student = slope[tile(t), :] + grid_sum(t, 1)
        residual = student - teach_ref[tile(t), :].astype(F32)
        weighted = area_ref[tile(t), :] * residual
        grad = 2.0 * weighted * inv_energy
        slope[tile(t), :] = grad
        slope_half[tile(t), :] = grad.astype(BF16)
        return acc + jnp.sum(weighted * residual, axis=0, keepdims=True)

    acc = lax.fori_loop(0, tiles, slope_tile, jnp.zeros((1, width), F32))
    mbuf[me] = folded(acc)

    back_decoded = to_mesh(slope_half, 2)
    c_gpd = exchanged((back_decoded * silu_slope(pre_dec[...])).astype(BF16), gpd, gpdo, base + 5)
    for c in w_copies:
        c.wait_recv()
    part = nt(gpd[...], decw_ref[own, :])
    c_gpd.wait_recv()
    bu[...] = part + nt(gpdo[...], deco[...])
    tbuf[...] = nn(cmt[...], bu[...].astype(BF16)).reshape(shards, PAD, width)
    rbuf[sid] = tbuf[sid]
    t_start()

    pg[own, :] = tn(upd[...], gpd[...]).astype(pg.dtype)
    pg[oth, :] = tn(updo[...], gpd[...]).astype(pg.dtype)
    if scatter_here:
        share = pg.shape[0] // shards
        g_start, g_recv, g_sent = spread(
            lambda i: pg.at[pl.ds(pl.multiple_of(i * share, 2 * PAD), share)], gbuf, gsend, grecv, shards, True
        )
        g_start()
        gbuf[sid] = pg[pl.ds(pl.multiple_of(sid * share, 2 * PAD), share), :]
    t_recv()

    bp[...] = bu[...]
    bp[0:PAD, :] = bu[0:PAD, :] + jnp.sum(rbuf[...], axis=0)
    c_gpp = exchanged((bp[...] * silu_slope(pre_proc[...])).astype(BF16), gpp, gppo, base + 6)
    part = bu[...] + nt(gpp[...], procw_ref[own, :])
    c_gpp.wait_recv()
    back_mesh = (part + nt(gppo[...], proco[...])).astype(BF16)
    stateo[...] = back_mesh
    send_messages(stateo[...], 3)
    m_start()

    def local_back(t):
        back[tile(t), :] = nn(amt[tile(t), :], stateo[...])
        pre_enc[tile(t), :] = silu_slope(pre_enc[tile(t), :])

    loop(tiles, local_back)
    route_recv(3, -1)

    def back_tile(t):
        total = back[tile(t), :] + grid_sum(t, 3)
        gpe[tile(t), :] = (total * pre_enc[tile(t), :]).astype(BF16)
        g_copy(t).start()

    loop(tiles, back_tile)

    def grad_tile(t):
        part = slope[tile(t), :] + nt(gpe[tile(t), :], encw_ref[own, :])
        g_copy(t).wait_recv()
        gx_ref[tile(t), :] = (part + nt(gpeo[tile(t), :], enco[...])).astype(BF16)

    loop(tiles, grad_tile)
    m_recv()
    misfit = jnp.sum(jnp.sum(mbuf[...], axis=0), keepdims=True)
    loss_ref[0] = jnp.sum(misfit * inv_energy)
    if scatter_here:
        g_recv()
        gd_ref[...] = jnp.sum(gbuf[...].astype(F32), axis=0)
        g_sent()
    else:
        gd_ref[...] = pg[...]

    def x_sent(t):
        x_copy(t).wait_send()
        g_copy(t).wait_send()

    loop(tiles, x_sent)
    for c in w_copies + [c_state, c_upd, c_gpd, c_gpp]:
        c.wait_send()
    route_sent(0, 1)
    route_sent(1, -1)
    route_sent(2, 1)
    route_sent(3, -1)
    for done in (e_sent, m_sent, c_sent, t_sent):
        done()


def on_device(
    nlat, nlon,
    grid_latent, teacher, mesh_init, enc_weight, proc_weight, dec_weight,
    local_grid, local_mesh, local_weight, send_row, send_count, recv_row, recv_weight,
    coarse_index, coarse_weight,
):
    rows, width = grid_latent.shape
    mrows = mesh_init.shape[0]
    full = enc_weight.shape[0]
    cap = send_row.shape[1]
    edges = local_grid.shape[0]
    shards = nlat * nlon
    nd = 2 * shards
    tiles = rows // TILE
    share = full // shards
    scatter_here = share % (2 * PAD) == 0
    slots = NB * cap

    slot_ids = jnp.arange(cap, dtype=jnp.int32)
    live = slot_ids[None, :] < send_count[:, None]
    send = jnp.where(live, send_row, -1)
    operands = (
        grid_latent, teacher, mesh_init, enc_weight, proc_weight, dec_weight,
        local_grid.reshape(1, edges), local_mesh.reshape(1, edges), local_weight.reshape(1, edges),
        send, recv_row, recv_weight, coarse_index.T, coarse_weight.T,
    )
    dma = pltpu.SemaphoreType.DMA
    V = pltpu.VMEM
    big = (rows, width)
    mid = (mrows, width)
    scratch = [
        V(big, BF16), V((width, width), BF16), V((width, width), BF16), V((width, width), BF16),
        V((mrows, edges), BF16), V((rows, edges), BF16), V((mrows, rows), BF16), V((rows, mrows), BF16),
        V((slots, rows), BF16), V((rows, slots), BF16), V((mrows, slots), BF16), V((slots, mrows), BF16),
        V((PAD * shards, mrows), BF16), V((rows, 1), F32), V((slots, 1), F32),
        V(big, F32), V(big, BF16), V(big, F32), V(big, BF16), V(big, BF16), V(big, BF16), V(big, F32),
        V((4, NB, cap, width), BF16), V((4, slots, width), BF16),
        V(mid, BF16), V(mid, BF16), V(mid, F32), V(mid, F32), V(mid, BF16), V(mid, BF16), V(mid, F32),
        V(mid, BF16), V(mid, BF16), V(mid, F32), V(mid, F32), V(mid, BF16), V(mid, BF16),
        V((nd, PAD, 128), F32), V((nd, PAD, 128), F32), V((shards, PAD, width), F32),
        V((shards, PAD, width), F32), V((shards, PAD, width), F32),
        V((full, width), BF16 if scatter_here else F32), V((shards if scatter_here else 1, max(share, 2 * PAD), width), BF16),
        dma((2 * tiles + 7,)), dma((2 * tiles + 7,)), dma((4, NB)), dma((4, NB)),
        dma((nd,)), dma((nd,)), dma((nd,)), dma((nd,)),
        dma((shards,)), dma((shards,)), dma((shards,)), dma((shards,)), dma((shards,)), dma((shards,)),
    ]
    vmem = pl.BlockSpec(memory_space=pltpu.VMEM)
    loss, grad_x, grad_dec = pl.pallas_call(
        functools.partial(kernel, nlat, nlon, scatter_here),
        out_shape=(
            jax.ShapeDtypeStruct((1,), F32),
            jax.ShapeDtypeStruct(big, BF16),
            jax.ShapeDtypeStruct((share if scatter_here else full, width), F32),
        ),
        in_specs=[vmem] * len(operands),
        out_specs=(pl.BlockSpec(memory_space=pltpu.SMEM), vmem, vmem),
        scratch_shapes=scratch,
        compiler_params=pltpu.CompilerParams(
            collective_id=0, has_side_effects=True, vmem_limit_bytes=(58 if shards <= 16 else 63) * 2**20
        ),
    )(*operands)
    if not scatter_here:
        grad_dec = lax.psum_scatter(grad_dec, ("lat", "lon"), scatter_dimension=0, tiled=True)
    return (loss, grad_x, grad_dec)


def solution(mesh):
    rows = P(("groups", "lat", "lon"), "feat")
    cols = P(None, "feat")
    flat = P(("lat", "lon"))
    table = P(("lat", "lon"), None)
    return jax.shard_map(
        functools.partial(on_device, mesh.shape["lat"], mesh.shape["lon"]),
        mesh=mesh,
        in_specs=(rows,) * 3 + (cols,) * 3 + (flat,) * 3 + (table, flat, table, table, table, table),
        out_specs=(P("groups"), rows, rows),
        check_vma=False,
    )
```
